32 devices in a mesh: space: 8 (over z, y), sub: 4 (over x, core).
Axes of the slice: x: 2, y: 2, z: 4, core: 2. Of those that a mesh axis runs over, the one named last changes fastest.
Arguments:
- rhs: bfloat16 [4096, 1024], P(('space', 'sub')), may hold values from -6 to 6
- blocks: bfloat16 [4096, 7, 4096], P(('space', 'sub')), may hold values from -0.125 to 0.125
- columns: int32 [4096, 7], P(('space', 'sub')), may hold values from 0 to 639, as said below
- ghost_lists: int32 [32, 128], P(('space', 'sub')), may hold values from 0 to 127, as said below
Outputs:
- solution: float32 [4096, 1024], P(('space', 'sub'))
- residual: float32 [4096, 1024], P(('space', 'sub'))
The draws below stay inside these ranges and needn't reach their ends.
Inputs may be any that keep to these rules, and one draw needn't show every extreme that they name: `columns`: for block row r (local) of device (p, q): entry 0 is q * 128 + r; entries 1 and 2 are q2 * 128 + ghost_lists[p * 4 + q2, k] for some q2 < 4 and k < 64; entries 3 and 4 lie in the part received from the previous subdomain, entries 5 and 6 in that from the next. `ghost_lists`: each row is a permutation of 0 .. 127.
All inputs are finite; a program needn't handle non-finite values.
Results may differ from the reference program's by a relative error of at most 0.0055.
Values may be sent and summed in bfloat16 or wider, within the bound.
A program may use at most 128 MiB of HBM per device.

```python
import jax
import jax.numpy as jnp
from jax import lax

BS = 64
NRHS = 16
NNZ = 7
S = 4
ROWS = 128
GHOST = 64
NBLOCKS = 4096
N_SPACE = 8
N_SUB = 4


def device_orders(key):
    keys = jax.random.split(jax.random.fold_in(key, 7), N_SPACE * N_SUB)
    return jax.vmap(lambda k: jax.random.permutation(k, ROWS))(keys).astype(jnp.int32)


def draw_ghost_lists(key, part):
    return device_orders(key)


def draw_columns(key, part):
    orders = device_orders(key)
    idx = jnp.arange(NBLOCKS, dtype=jnp.int32)
    local = idx % ROWS
    device = idx // ROWS
    sub_idx = device % N_SUB
    base_dev = device - sub_idx
    sub_len = N_SUB * ROWS
    keys = jax.random.split(jax.random.fold_in(key, 11), 8)
    first = sub_idx * ROWS + local
    peer_a = jax.random.randint(keys[0], (NBLOCKS,), 0, N_SUB)
    slot_a = jax.random.randint(keys[1], (NBLOCKS,), 0, GHOST)
    peer_b = jax.random.randint(keys[6], (NBLOCKS,), 0, N_SUB)
    slot_b = jax.random.randint(keys[7], (NBLOCKS,), 0, GHOST)
    near_a = peer_a * ROWS + orders[base_dev + peer_a, slot_a]
    near_b = peer_b * ROWS + orders[base_dev + peer_b, slot_b]
    offset_low = jax.random.randint(keys[2], (N_SPACE * N_SUB,), 0, GHOST)[device]
    offset_high = jax.random.randint(keys[3], (N_SPACE * N_SUB,), 0, GHOST)[device]
    low_a = sub_len + (local + offset_low) % GHOST
    low_b = sub_len + jax.random.randint(keys[4], (NBLOCKS,), 0, GHOST)
    high_a = sub_len + GHOST + (local + offset_high) % GHOST
    high_b = sub_len + GHOST + jax.random.randint(keys[5], (NBLOCKS,), 0, GHOST)
    return jnp.stack([first, near_a, near_b, low_a, low_b, high_a, high_b], axis=1).astype(jnp.int32)


def steps_of(key, dims, pieces, least, top_value):
    gain = 1.0
    for dim, parts in pieces:
        draws = jax.random.uniform(jax.random.fold_in(jax.random.fold_in(key, 6), dim), (parts,), jnp.float32, least / len(pieces), top_value / len(pieces))
        gain = gain * jnp.repeat(jnp.exp(draws), dims[dim] // parts).reshape((-1,) + (1,) * (len(dims) - 1 - dim))
    return gain


def bell_draw(own_key, dims, scale, limit, shards=(), kind=jnp.bfloat16):
    loudness = steps_of(own_key, dims, shards, -0.22, 0.18) if shards else 1.0
    result = jax.random.normal(own_key, dims, jnp.float32) * scale * loudness
    return jnp.minimum(jnp.maximum(result, -limit), limit).astype(kind)


def setup_inputs(seed: int = 0) -> dict:
    arg_keys = jax.random.split(jax.random.key(seed), 5)
    return {
        "rhs": bell_draw(arg_keys[0], (NBLOCKS, BS * NRHS), 1.0, 6.0, ((0, 32),)),
        "blocks": bell_draw(arg_keys[1], (NBLOCKS, NNZ, BS * BS), (4 * NNZ * BS) ** -0.5, 0.125, ((0, 32),)),
        "columns": draw_columns(jax.random.fold_in(arg_keys[4], 71), 0),
        "ghost_lists": draw_ghost_lists(jax.random.fold_in(arg_keys[4], 71), 0),
    }


def ext_index(ghost_lists):
    devs = N_SPACE * N_SUB
    sub_len = N_SUB * ROWS
    dev = jnp.arange(devs, dtype=jnp.int32)
    space_idx = dev // N_SUB
    own = space_idx[:, None] * sub_len + jnp.arange(sub_len, dtype=jnp.int32)[None, :]
    below = jnp.clip(dev - N_SUB, 0, devs - 1)
    above = jnp.clip(dev + N_SUB, 0, devs - 1)
    low_rows = below[:, None] * ROWS + ghost_lists[below][:, :GHOST]
    high_rows = above[:, None] * ROWS + ghost_lists[above][:, GHOST:]
    low_ok = jnp.broadcast_to((space_idx > 0)[:, None], low_rows.shape)
    high_ok = jnp.broadcast_to((space_idx < N_SPACE - 1)[:, None], high_rows.shape)
    table = jnp.concatenate([own, low_rows, high_rows], axis=1).astype(jnp.int32)
    valid = jnp.concatenate([jnp.ones(own.shape, bool), low_ok, high_ok], axis=1)
    return (table, valid)

def reference(rhs, blocks, columns, ghost_lists):
    table, valid = ext_index(ghost_lists)
    owner = (jnp.arange(NBLOCKS, dtype=jnp.int32) // ROWS).astype(jnp.int32)
    global_cols = table[owner[:, None], columns]
    weight = valid[owner[:, None], columns].astype(jnp.float32)
    basis = [rhs]
    for j in range(S):
        cur = basis[-1].reshape(NBLOCKS, BS, NRHS).astype(jnp.float32)
        total = jnp.zeros((NBLOCKS, BS, NRHS), jnp.float32)
        for b in range(NNZ):
            picked = cur[global_cols[:, b]] * weight[:, b][:, None, None]
            mats = blocks[:, b].reshape(NBLOCKS, BS, BS).astype(jnp.float32)
            total = total + jnp.einsum('rij,rjk->rik', mats, picked)
        basis.append(total.astype(jnp.bfloat16).reshape(NBLOCKS, BS * NRHS))
    stack = jnp.stack(basis, axis=1).reshape(NBLOCKS, S + 1, BS, NRHS)
    gram = jnp.einsum('rjia,rkic->jakc', stack.astype(jnp.float32), stack.astype(jnp.float32), preferred_element_type=jnp.float32)
    sol, res = finish(rhs, stack, gram)
    return (sol, res)

def finish(rhs, stack, gram):
    rows = stack.shape[0]
    paired = gram[1:] + gram[:-1]
    hmat = (paired[:, :, 1:] + paired[:, :, :-1]).reshape(S * NRHS, S * NRHS)
    cvec = paired[:, :, 0].reshape(S * NRHS, NRHS)
    lower = jnp.linalg.cholesky(hmat)
    coef = jax.scipy.linalg.cho_solve((lower, True), cvec).reshape(S, NRHS, NRHS)
    kfull = stack.astype(jnp.float32)
    hi = lax.Precision.HIGHEST
    sol = jnp.einsum('rjia,jac->ric', kfull[:, :S], coef, precision=hi)
    wmat = kfull[:, 1:] + kfull[:, :S]
    image = jnp.einsum('rjia,jac->ric', wmat, coef, precision=hi)
    res = rhs.astype(jnp.float32).reshape(rows, BS, NRHS) - image
    return (sol.reshape(rows, BS * NRHS), res.reshape(rows, BS * NRHS))
```

```python
import functools

import jax
import jax.numpy as jnp
from jax import lax
from jax.experimental import pallas as pl
from jax.experimental.pallas import tpu as pltpu
from jax.sharding import PartitionSpec as P

BS = 64
NRHS = 16
NNZ = 7
S = 4
MESH = pl.DeviceIdType.MESH
NT = (((1,), (1,)), ((), ()))
CHUNKS = 4


def log2(n):
    return n.bit_length() - 1


def powers_kernel(
    n_space, n_sub, rows, ghost,
    index_ref, list_ref, first_ref, blocks_ref,
    gram_ref, basis_ref,
    raw, mats, turn, ext, fresh, up, down, near, low, high, gsend, grecv,
    load_sem, send_sem, recv_sem, gsend_sem, grecv_sem,
):
    p = lax.axis_index("space")
    q = lax.axis_index("sub")
    half = ghost // 2
    pairs = rows // 2
    rounds_sub, rounds_space = log2(n_sub), log2(n_space)
    has_low = p > 0
    has_high = p < n_space - 1

    per = rows // CHUNKS
    loads = [
        pltpu.make_async_copy(
            blocks_ref.at[pl.ds(n * per, per)], raw.at[pl.ds(n * per, per)], load_sem.at[n]
        )
        for n in range(CHUNKS)
    ]
    for load in loads:
        load.start()

    def flip(index, step):
        return index + step * (1 - 2 * ((index // step) % 2))

    barrier = pltpu.get_barrier_semaphore()
    for d in range(1, n_sub):
        pl.semaphore_signal(barrier, inc=1, device_id=(p, (q + d) % n_sub), device_id_type=MESH)
    for r in range(1, rounds_space):
        pl.semaphore_signal(barrier, inc=1, device_id=(flip(p, 1 << r), q), device_id_type=MESH)

    @pl.when(has_low)
    def _():
        pl.semaphore_signal(barrier, inc=1, device_id=(p - 1, q), device_id_type=MESH)

    @pl.when(has_high)
    def _():
        pl.semaphore_signal(barrier, inc=1, device_id=(p + 1, q), device_id_type=MESH)

    left16 = lax.broadcasted_iota(jnp.int32, (NRHS, 128), 1) < BS
    left32 = lax.broadcasted_iota(jnp.int32, (32, 128), 1) < BS
    src = lax.broadcasted_iota(jnp.int32, (128, 256), 0)
    dst = lax.broadcasted_iota(jnp.int32, (128, 256), 1)
    src_c = 2 * (src % 32) + (src // 32) % 2
    order = jnp.where((src // BS == dst // 128) & (src_c == dst % BS), 1.0, 0.0).astype(jnp.bfloat16)
    double = jnp.where((src // BS == dst // 128) & (src % BS == dst % BS), 1.0, 0.0).astype(jnp.bfloat16)

    def own_start(m, carry):
        even, odd = first_ref[2 * m], first_ref[2 * m + 1]
        ext[2 * m] = even
        ext[2 * m + 1] = odd
        basis_ref[0, m] = jnp.where(left16, even, odd)
        return carry

    lax.fori_loop(0, pairs, own_start, 0)

    def zero(m, carry):
        ext[rows + n_sub * ghost + m] = jnp.zeros((NRHS, 128), jnp.bfloat16)
        return carry

    lax.fori_loop(0, 2 * ghost, zero, 0)

    def copies(j):
        near_copies = [
            pltpu.make_async_remote_copy(
                src_ref=up.at[j], dst_ref=near.at[j, d - 1],
                send_sem=send_sem.at[j, d - 1], recv_sem=recv_sem.at[j, d - 1],
                device_id=(p, (q + d) % n_sub), device_id_type=MESH,
            )
            for d in range(1, n_sub)
        ]
        up_copy = pltpu.make_async_remote_copy(
            src_ref=up.at[j], dst_ref=low.at[j],
            send_sem=send_sem.at[j, n_sub - 1], recv_sem=recv_sem.at[j, n_sub - 1],
            device_id=((p + 1) % n_space, q), device_id_type=MESH,
        )
        down_copy = pltpu.make_async_remote_copy(
            src_ref=down.at[j], dst_ref=high.at[j],
            send_sem=send_sem.at[j, n_sub], recv_sem=recv_sem.at[j, n_sub],
            device_id=((p + n_space - 1) % n_space, q), device_id_type=MESH,
        )
        return near_copies, up_copy, down_copy

    def send(j):
        near_copies, up_copy, down_copy = copies(j)

        def pack_up(m, carry):
            up[j, m] = jnp.where(left16, ext[list_ref[2 * m]], ext[list_ref[2 * m + 1]])
            return carry

        def pack_down(m, carry):
            down[j, m] = jnp.where(
                left16, ext[list_ref[ghost + 2 * m]], ext[list_ref[ghost + 2 * m + 1]]
            )
            return carry

        lax.fori_loop(0, half, pack_up, 0, unroll=4)
        if j == 0:
            greeted = (n_sub - 1) + (rounds_space - 1)
            pl.semaphore_wait(barrier, greeted + jnp.where(has_low, 1, 0) + jnp.where(has_high, 1, 0))
        pl.when(has_high)(up_copy.start)
        for copy in near_copies:
            copy.start()
        lax.fori_loop(0, half, pack_down, 0, unroll=4)
        pl.when(has_low)(down_copy.start)

    def spread(buffer, lead, base):
        def body(m, carry):
            part = buffer[lead + (pl.ds(4 * m, 4),)].reshape(4 * NRHS, 128)
            wide = jnp.dot(part, double, preferred_element_type=jnp.float32).astype(jnp.bfloat16)
            for h in range(4):
                rows_h = wide[h * NRHS:(h + 1) * NRHS]
                ext[base + 8 * m + 2 * h] = rows_h[:, :128]
                ext[base + 8 * m + 2 * h + 1] = rows_h[:, 128:]
            return carry

        lax.fori_loop(0, half // 4, body, 0)

    def receive(j):
        near_copies, up_copy, down_copy = copies(j)
        for d, copy in enumerate(near_copies):
            copy.wait_recv()
            spread(near, (j, d), rows + d * ghost)

        @pl.when(has_low)
        def _():
            up_copy.wait_recv()
            spread(low, (j,), rows + n_sub * ghost)

        @pl.when(has_high)
        def _():
            down_copy.wait_recv()
            spread(high, (j,), rows + n_sub * ghost + ghost)

    def sent(j):
        near_copies, up_copy, down_copy = copies(j)
        for copy in near_copies:
            copy.wait_send()
        pl.when(has_high)(up_copy.wait_send)
        pl.when(has_low)(down_copy.wait_send)

    def relay(i, carry):
        for t in range(32):
            turn[t * 8:t * 8 + NNZ, :] = raw[i, :, t * 128:(t + 1) * 128].astype(jnp.float32)
        planes = [turn[pl.ds(b, 32, stride=8), :] for b in range(NNZ)]
        swapped = [pltpu.roll(plane, BS, 1) for plane in planes]
        zeros = jnp.zeros((32, 128), jnp.float32)
        planes.append(zeros)
        swapped.append(zeros)
        for m in range(4):
            a, b = 2 * m, 2 * m + 1
            mats[i, 0:32, m * 128:(m + 1) * 128] = jnp.where(left32, planes[a], swapped[b]).astype(jnp.bfloat16)
            mats[i, 32:64, m * 128:(m + 1) * 128] = jnp.where(left32, swapped[a], planes[b]).astype(jnp.bfloat16)
        return carry

    def product(j):
        def body(g, carry):
            lines = []
            for u in range(4):
                at = (4 * g + u) * NNZ
                tiles = [ext[index_ref[at + b]] for b in range(NNZ)]
                lines.append(jnp.concatenate(
                    [jnp.where(left16, tiles[2 * m], tiles[2 * m + 1]) for m in range(3)] + [tiles[6]], axis=1
                ))
            lhs = jnp.concatenate(lines, axis=0)
            rhs = mats[pl.ds(4 * g, 4)].reshape(4 * BS, 512)
            full = lax.dot_general(lhs, rhs, NT, preferred_element_type=jnp.float32)
            left = left16
            picked = [
                jnp.where(
                    left,
                    full[2 * h * NRHS:(2 * h + 1) * NRHS, h * 128:(h + 1) * 128],
                    full[(2 * h + 1) * NRHS:(2 * h + 2) * NRHS, h * 128:(h + 1) * 128],
                ).astype(jnp.bfloat16)
                for h in range(2)
            ]
            wide = jnp.dot(
                jnp.concatenate(picked, axis=0), order, preferred_element_type=jnp.float32
            ).astype(jnp.bfloat16)
            for h in range(2):
                even = wide[h * NRHS:(h + 1) * NRHS, :128]
                odd = wide[h * NRHS:(h + 1) * NRHS, 128:]
                fresh[4 * g + 2 * h] = even
                fresh[4 * g + 2 * h + 1] = odd
                basis_ref[j + 1, 2 * g + h] = jnp.where(left16, even, odd)
            return carry

        lax.fori_loop(0, rows // 4, body, 0)

        def take(m, carry):
            ext[m] = fresh[m]
            return carry

        if j < S - 1:
            lax.fori_loop(0, rows, take, 0, unroll=8)

    for j in range(S):
        send(j)
        if j == 0:
            for n in range(CHUNKS):
                loads[n].wait()
                lax.fori_loop(n * per, (n + 1) * per, relay, 0)
        receive(j)
        product(j)
        sent(j)

    width = (S + 1) * NRHS

    def gram_step(m, total):
        tile = jnp.concatenate(
            [basis_ref[:, 2 * m + h].reshape(width, 128) for h in range(2)], axis=1
        )
        return total + lax.dot_general(tile, tile, NT, preferred_element_type=jnp.float32)

    total = lax.fori_loop(0, pairs // 2, gram_step, jnp.zeros((width, width), jnp.float32))
    rounds = rounds_sub + rounds_space
    gsend[...] = jnp.zeros_like(gsend)
    gsend[0, :, :width] = total
    for r in range(rounds):
        if r < rounds_sub:
            partner = (p, flip(q, 1 << r))
        else:
            partner = (flip(p, 1 << (r - rounds_sub)), q)
        copy = pltpu.make_async_remote_copy(
            src_ref=gsend.at[r], dst_ref=grecv.at[r],
            send_sem=gsend_sem.at[r], recv_sem=grecv_sem.at[r],
            device_id=partner, device_id_type=MESH,
        )
        copy.start()
        copy.wait()
        if r < rounds - 1:
            gsend[r + 1] = gsend[r] + grecv[r]
        else:
            gram_ref[...] = gsend[r] + grecv[r]


def powers(n_space, n_sub, index, lists, first, blocks):
    rows = blocks.shape[0]
    ghost = lists.shape[0] // 2
    half = ghost // 2
    width = (S + 1) * NRHS
    rounds = log2(n_sub) + log2(n_space)
    bf, f32 = jnp.bfloat16, jnp.float32
    return pl.pallas_call(
        functools.partial(powers_kernel, n_space, n_sub, rows, ghost),
        out_shape=(
            jax.ShapeDtypeStruct((width, 128), f32),
            jax.ShapeDtypeStruct((S + 1, rows // 2, NRHS, 128), bf),
        ),
        in_specs=[
            pl.BlockSpec(memory_space=pltpu.SMEM),
            pl.BlockSpec(memory_space=pltpu.SMEM),
            pl.BlockSpec(memory_space=pltpu.VMEM),
            pl.BlockSpec(memory_space=pl.ANY),
        ],
        out_specs=[pl.BlockSpec(memory_space=pltpu.VMEM)] * 2,
        scratch_shapes=[
            pltpu.VMEM((rows, NNZ, BS * BS), bf),
            pltpu.VMEM((rows, BS, 512), bf),
            pltpu.VMEM((256, 128), f32),
            pltpu.VMEM((rows + n_sub * ghost + 2 * ghost, NRHS, 128), bf),
            pltpu.VMEM((rows, NRHS, 128), bf),
            pltpu.VMEM((S, half, NRHS, 128), bf),
            pltpu.VMEM((S, half, NRHS, 128), bf),
            pltpu.VMEM((S, n_sub - 1, half, NRHS, 128), bf),
            pltpu.VMEM((S, half, NRHS, 128), bf),
            pltpu.VMEM((S, half, NRHS, 128), bf),
            pltpu.VMEM((rounds, width, 128), f32),
            pltpu.VMEM((rounds, width, 128), f32),
            pltpu.SemaphoreType.DMA((CHUNKS,)),
            pltpu.SemaphoreType.DMA((S, n_sub + 1)),
            pltpu.SemaphoreType.DMA((S, n_sub + 1)),
            pltpu.SemaphoreType.DMA((rounds,)),
            pltpu.SemaphoreType.DMA((rounds,)),
        ],
        compiler_params=pltpu.CompilerParams(
            collective_id=0, has_side_effects=True, vmem_limit_bytes=56 * 1024 * 1024
        ),
    )(index, lists, first, blocks)


def finish(rhs, stack, gram):
    rows = stack.shape[0]
    paired = gram[1:] + gram[:-1]
    hmat = (paired[:, :, 1:] + paired[:, :, :-1]).reshape(S * NRHS, S * NRHS)
    cvec = paired[:, :, 0].reshape(S * NRHS, NRHS)
    lower = jnp.linalg.cholesky(hmat)
    coef = jax.scipy.linalg.cho_solve((lower, True), cvec).reshape(S, NRHS, NRHS)
    kfull = stack.astype(jnp.float32)
    highest = lax.Precision.HIGHEST
    sol = jnp.einsum("rjia,jac->ric", kfull[:, :S], coef, precision=highest)
    wmat = kfull[:, 1:] + kfull[:, :S]
    image = jnp.einsum("rjia,jac->ric", wmat, coef, precision=highest)
    res = rhs.astype(jnp.float32).reshape(rows, BS, NRHS) - image
    return (sol.reshape(rows, BS * NRHS), res.reshape(rows, BS * NRHS))


def on_device(rhs, blocks, columns, ghost_lists):
    n_space, n_sub = lax.axis_size("space"), lax.axis_size("sub")
    rows = rhs.shape[0]
    ghost = ghost_lists.shape[1] // 2
    q = lax.axis_index("sub")
    lists = ghost_lists[0]
    every = lax.all_gather(lists, "sub", axis=0)
    near = columns[:, 1:3]
    peer, row = near // rows, near % rows
    owner = jnp.arange(n_sub, dtype=jnp.int32)
    match = (peer[..., None, None] == owner[:, None]) & (row[..., None, None] == every[:, :ghost])
    place = jnp.sum(jnp.where(match, jnp.arange(ghost, dtype=jnp.int32), 0), axis=(2, 3))
    slot = (q - peer - 1) % n_sub
    near = jnp.where(peer == q, row, rows + slot * ghost + place)
    far = columns[:, 3:] - n_sub * rows + rows + n_sub * ghost
    local = jnp.arange(rows, dtype=jnp.int32)[:, None]
    index = jnp.concatenate([local, near, far], axis=1).reshape(-1)
    first = rhs.reshape(rows, BS, NRHS).transpose(0, 2, 1)
    first = jnp.concatenate([first, first], axis=2)
    gram, basis = powers(n_space, n_sub, index, lists, first, blocks)
    width = (S + 1) * NRHS
    gram = gram[:, :width].reshape(S + 1, NRHS, S + 1, NRHS)
    stack = basis.reshape(S + 1, rows // 2, NRHS, 2, BS).transpose(1, 3, 0, 4, 2)
    return finish(rhs, stack.reshape(rows, S + 1, BS, NRHS), gram)


def solution(mesh):
    in_specs = (
        P(("space", "sub"), None),
        P(("space", "sub"), None, None),
        P(("space", "sub"), None),
        P(("space", "sub"), None),
    )
    out_specs = (P(("space", "sub"), None), P(("space", "sub"), None))
    return jax.shard_map(
        on_device, mesh=mesh, in_specs=in_specs, out_specs=out_specs, check_vma=False
    )
```

```python
import functools

import jax
import jax.numpy as jnp
from jax import lax
from jax.experimental import pallas as pl
from jax.experimental.pallas import tpu as pltpu
from jax.sharding import PartitionSpec as P

BS = 64
NRHS = 16
NNZ = 7
S = 4
MESH = pl.DeviceIdType.MESH
NT = (((1,), (1,)), ((), ()))
CHUNKS = 4


def log2(n):
    return n.bit_length() - 1


def powers_kernel(
    n_space, n_sub, rows, ghost,
    index_ref, list_ref, first_ref, blocks_ref,
    gram_ref, nat_ref,
    basis, lined, tall, perm, raw, mats, turn, ext, fresh, up, down, near, low, high, gsend, grecv,
    load_sem, send_sem, recv_sem, gsend_sem, grecv_sem,
):
    p = lax.axis_index("space")
    q = lax.axis_index("sub")
    half = ghost // 2
    pairs = rows // 2
    rounds_space = log2(n_space)
    has_low = p > 0
    flat = BS * NRHS
    has_high = p < n_space - 1

    per = rows // CHUNKS
    loads = [
        pltpu.make_async_copy(
            blocks_ref.at[:, pl.ds(n * per, per)], raw.at[:, pl.ds(n * per, per)], load_sem.at[n]
        )
        for n in range(CHUNKS)
    ]
    for load in loads:
        load.start()

    def flip(index, step):
        return index + step * (1 - 2 * ((index // step) % 2))

    barrier = pltpu.get_barrier_semaphore()
    for d in range(1, n_sub):
        pl.semaphore_signal(barrier, inc=1, device_id=(p, (q + d) % n_sub), device_id_type=MESH)
    for r in range(1, rounds_space):
        pl.semaphore_signal(barrier, inc=1, device_id=(flip(p, 1 << r), q), device_id_type=MESH)

    @pl.when(has_low)
    def _():
        pl.semaphore_signal(barrier, inc=1, device_id=(p - 1, q), device_id_type=MESH)

    @pl.when(has_high)
    def _():
        pl.semaphore_signal(barrier, inc=1, device_id=(p + 1, q), device_id_type=MESH)

    left16 = lax.broadcasted_iota(jnp.int32, (NRHS, 128), 1) < BS
    left32 = lax.broadcasted_iota(jnp.int32, (32, 128), 1) < BS
    src = lax.broadcasted_iota(jnp.int32, (128, 256), 0)
    dst = lax.broadcasted_iota(jnp.int32, (128, 256), 1)
    src_c = 2 * (src % 32) + (src // 32) % 2
    order = jnp.where((src // BS == dst // 128) & (src_c == dst % BS), 1.0, 0.0).astype(jnp.bfloat16)
    double = jnp.where((src // BS == dst // 128) & (src % BS == dst % BS), 1.0, 0.0).astype(jnp.bfloat16)

    def own_start(m, carry):
        even, odd = first_ref[2 * m], first_ref[2 * m + 1]
        ext[2 * m] = even
        ext[2 * m + 1] = odd
        basis[0, m] = jnp.where(left16, even, odd)
        return carry

    lax.fori_loop(0, pairs, own_start, 0)

    def zero(m, carry):
        ext[rows + n_sub * ghost + m] = jnp.zeros((NRHS, 128), jnp.bfloat16)
        return carry

    lax.fori_loop(0, 2 * ghost, zero, 0)

    def copies(j):
        near_copies = [
            pltpu.make_async_remote_copy(
                src_ref=up.at[j], dst_ref=near.at[j, d - 1],
                send_sem=send_sem.at[j, d - 1], recv_sem=recv_sem.at[j, d - 1],
                device_id=(p, (q + d) % n_sub), device_id_type=MESH,
            )
            for d in range(1, n_sub)
        ]
        up_copy = pltpu.make_async_remote_copy(
            src_ref=up.at[j], dst_ref=low.at[j],
            send_sem=send_sem.at[j, n_sub - 1], recv_sem=recv_sem.at[j, n_sub - 1],
            device_id=((p + 1) % n_space, q), device_id_type=MESH,
        )
        down_copy = pltpu.make_async_remote_copy(
            src_ref=down.at[j], dst_ref=high.at[j],
            send_sem=send_sem.at[j, n_sub], recv_sem=recv_sem.at[j, n_sub],
            device_id=((p + n_space - 1) % n_space, q), device_id_type=MESH,
        )
        return near_copies, up_copy, down_copy

    def send(j):
        near_copies, up_copy, down_copy = copies(j)

        def pack_up(m, carry):
            up[j, m] = jnp.where(left16, ext[list_ref[2 * m]], ext[list_ref[2 * m + 1]])
            return carry

        def pack_down(m, carry):
            down[j, m] = jnp.where(
                left16, ext[list_ref[ghost + 2 * m]], ext[list_ref[ghost + 2 * m + 1]]
            )
            return carry

        lax.fori_loop(0, half, pack_up, 0, unroll=4)
        if j == 0:
            greeted = (n_sub - 1) + (rounds_space - 1)
            pl.semaphore_wait(barrier, greeted + jnp.where(has_low, 1, 0) + jnp.where(has_high, 1, 0))
        pl.when(has_high)(up_copy.start)
        for copy in near_copies:
            copy.start()
        lax.fori_loop(0, half, pack_down, 0, unroll=4)
        pl.when(has_low)(down_copy.start)

    def spread(buffer, lead, base):
        def body(m, carry):
            part = buffer[lead + (pl.ds(4 * m, 4),)].reshape(4 * NRHS, 128)
            wide = jnp.dot(part, double, preferred_element_type=jnp.float32).astype(jnp.bfloat16)
            for h in range(4):
                rows_h = wide[h * NRHS:(h + 1) * NRHS]
                ext[base + 8 * m + 2 * h] = rows_h[:, :128]
                ext[base + 8 * m + 2 * h + 1] = rows_h[:, 128:]
            return carry

        lax.fori_loop(0, half // 4, body, 0, unroll=8)

    def receive(j):
        near_copies, up_copy, down_copy = copies(j)
        for d, copy in enumerate(near_copies):
            copy.wait_recv()
            spread(near, (j, d), rows + d * ghost)

        @pl.when(has_low)
        def _():
            up_copy.wait_recv()
            spread(low, (j,), rows + n_sub * ghost)

        @pl.when(has_high)
        def _():
            down_copy.wait_recv()
            spread(high, (j,), rows + n_sub * ghost + ghost)

    def sent(j):
        near_copies, up_copy, down_copy = copies(j)
        for copy in near_copies:
            copy.wait_send()
        pl.when(has_high)(up_copy.wait_send)
        pl.when(has_low)(down_copy.wait_send)

    def relay(g, carry):
        base = pl.multiple_of(g * 16, 16)
        for m in range(4):
            members = [b for b in (2 * m, 2 * m + 1) if b < NNZ]
            for b in members:
                for t in range(32):
                    turn[b % 2, t * 16:(t + 1) * 16, :] = raw[
                        b, pl.ds(base, 16), t * 128:(t + 1) * 128
                    ].astype(jnp.float32)
            for u in range(16):
                planes = [turn[b % 2, pl.ds(u, 32, stride=16), :] for b in members]
                swapped = [pltpu.roll(plane, BS, 1) for plane in planes]
                if len(members) < 2:
                    planes.append(jnp.zeros((32, 128), jnp.float32))
                    swapped.append(planes[1])
                lanes = slice(m * 128, (m + 1) * 128)
                mats[base + u, 0:32, lanes] = jnp.where(left32, planes[0], swapped[1]).astype(jnp.bfloat16)
                mats[base + u, 32:64, lanes] = jnp.where(left32, swapped[0], planes[1]).astype(jnp.bfloat16)
        return carry

    def product(j):
        def body(g, carry):
            lines = []
            for u in range(4):
                at = 4 * g + u
                tiles = [ext[index_ref[b, at]] for b in range(NNZ)]
                lines.append(jnp.concatenate(
                    [jnp.where(left16, tiles[2 * m], tiles[2 * m + 1]) for m in range(3)] + [tiles[6]], axis=1
                ))
            lhs = jnp.concatenate(lines, axis=0)
            rhs = mats[pl.ds(4 * g, 4)].reshape(4 * BS, 512)
            full = lax.dot_general(lhs, rhs, NT, preferred_element_type=jnp.float32)
            left = left16
            picked = [
                jnp.where(
                    left,
                    full[2 * h * NRHS:(2 * h + 1) * NRHS, h * 128:(h + 1) * 128],
                    full[(2 * h + 1) * NRHS:(2 * h + 2) * NRHS, h * 128:(h + 1) * 128],
                ).astype(jnp.bfloat16)
                for h in range(2)
            ]
            wide = jnp.dot(
                jnp.concatenate(picked, axis=0), order, preferred_element_type=jnp.float32
            ).astype(jnp.bfloat16)
            for h in range(2):
                even = wide[h * NRHS:(h + 1) * NRHS, :128]
                odd = wide[h * NRHS:(h + 1) * NRHS, 128:]
                fresh[4 * g + 2 * h] = even
                fresh[4 * g + 2 * h + 1] = odd
                basis[j + 1, 2 * g + h] = jnp.where(left16, even, odd)
            return carry

        lax.fori_loop(0, rows // 4, body, 0, unroll=4)

        def take(m, carry):
            ext[m] = fresh[m]
            return carry

        if j < S - 1:
            lax.fori_loop(0, rows, take, 0, unroll=8)

    def natural(j):
        def line(m, carry):
            base = pl.multiple_of(m * 32, 32)
            tall[...] = fresh[pl.ds(base, 32)].reshape(32 * NRHS, 128).astype(jnp.float32)
            planes = [tall[pl.ds(k, 32, stride=NRHS), :] for k in range(NRHS)]
            for k in range(NRHS // 2):
                lined[pl.ds(base, 32), k * 128:(k + 1) * 128] = jnp.where(
                    left32, planes[2 * k], planes[2 * k + 1]
                ).astype(jnp.bfloat16)
            return carry

        lax.fori_loop(0, rows // 32, line, 0)
        for n in range(flat // 256):
            lanes = slice(n * 256, (n + 1) * 256)
            nat_ref[j, :, lanes] = jnp.dot(
                lined[...], perm[:, lanes], preferred_element_type=jnp.float32
            ).astype(jnp.bfloat16)

    def permutation(k, carry):
        at = lax.broadcasted_iota(jnp.int32, (BS, flat), 1)
        c = lax.broadcasted_iota(jnp.int32, (BS, flat), 0)
        perm[pl.ds(pl.multiple_of(k * BS, BS), BS), :] = jnp.where(
            at == c * NRHS + k, 1.0, 0.0
        ).astype(jnp.bfloat16)
        return carry

    for j in range(S):
        send(j)
        if j == 1:
            lax.fori_loop(0, NRHS, permutation, 0)
        if j >= 1:
            natural(j - 1)
        if j == 0:
            for n in range(CHUNKS):
                loads[n].wait()
                lax.fori_loop(n * per // 16, (n + 1) * per // 16, relay, 0)
        receive(j)
        product(j)
        sent(j)

    width = (S + 1) * NRHS

    def gram_step(m, total):
        tile = jnp.concatenate(
            [basis[:, 8 * m + h].reshape(width, 128) for h in range(8)], axis=1
        )
        return total + lax.dot_general(tile, tile, NT, preferred_element_type=jnp.float32)

    total = lax.fori_loop(0, pairs // 8, gram_step, jnp.zeros((width, width), jnp.float32), unroll=2)
    gsend[...] = jnp.zeros_like(gsend)
    gsend[0, :, :width] = total
    peers = [
        pltpu.make_async_remote_copy(
            src_ref=gsend.at[0], dst_ref=grecv.at[d - 1],
            send_sem=gsend_sem.at[d - 1], recv_sem=grecv_sem.at[d - 1],
            device_id=(p, (q + d) % n_sub), device_id_type=MESH,
        )
        for d in range(1, n_sub)
    ]
    for copy in peers:
        copy.start()
    natural(S - 1)
    value = gsend[0]
    for d, copy in enumerate(peers):
        copy.wait()
        value = value + grecv[d]
    for r in range(rounds_space):
        at = n_sub - 1 + r
        gsend[r + 1] = value
        copy = pltpu.make_async_remote_copy(
            src_ref=gsend.at[r + 1], dst_ref=grecv.at[at],
            send_sem=gsend_sem.at[at], recv_sem=grecv_sem.at[at],
            device_id=(flip(p, 1 << r), q), device_id_type=MESH,
        )
        copy.start()
        copy.wait()
        value = value + grecv[at]
    gram_ref[...] = value


def powers(n_space, n_sub, index, lists, first, blocks):
    rows = blocks.shape[1]
    ghost = lists.shape[0] // 2
    half = ghost // 2
    width = (S + 1) * NRHS
    rounds = n_sub - 1 + log2(n_space)
    bf, f32 = jnp.bfloat16, jnp.float32
    return pl.pallas_call(
        functools.partial(powers_kernel, n_space, n_sub, rows, ghost),
        out_shape=(
            jax.ShapeDtypeStruct((width, 128), f32),
            jax.ShapeDtypeStruct((S, rows, BS * NRHS), bf),
        ),
        in_specs=[
            pl.BlockSpec(memory_space=pltpu.SMEM),
            pl.BlockSpec(memory_space=pltpu.SMEM),
            pl.BlockSpec(memory_space=pltpu.VMEM),
            pl.BlockSpec(memory_space=pl.ANY),
        ],
        out_specs=[pl.BlockSpec(memory_space=pltpu.VMEM)] * 2,
        scratch_shapes=[
            pltpu.VMEM((S + 1, rows // 2, NRHS, 128), bf),
            pltpu.VMEM((rows, BS * NRHS), bf),
            pltpu.VMEM((32 * NRHS, 128), f32),
            pltpu.VMEM((BS * NRHS, BS * NRHS), bf),
            pltpu.VMEM((NNZ, rows, BS * BS), bf),
            pltpu.VMEM((rows, BS, 512), bf),
            pltpu.VMEM((2, 512, 128), f32),
            pltpu.VMEM((rows + n_sub * ghost + 2 * ghost, NRHS, 128), bf),
            pltpu.VMEM((rows, NRHS, 128), bf),
            pltpu.VMEM((S, half, NRHS, 128), bf),
            pltpu.VMEM((S, half, NRHS, 128), bf),
            pltpu.VMEM((S, n_sub - 1, half, NRHS, 128), bf),
            pltpu.VMEM((S, half, NRHS, 128), bf),
            pltpu.VMEM((S, half, NRHS, 128), bf),
            pltpu.VMEM((rounds, width, 128), f32),
            pltpu.VMEM((rounds, width, 128), f32),
            pltpu.SemaphoreType.DMA((CHUNKS,)),
            pltpu.SemaphoreType.DMA((S, n_sub + 1)),
            pltpu.SemaphoreType.DMA((S, n_sub + 1)),
            pltpu.SemaphoreType.DMA((rounds,)),
            pltpu.SemaphoreType.DMA((rounds,)),
        ],
        compiler_params=pltpu.CompilerParams(
            collective_id=0, has_side_effects=True, vmem_limit_bytes=56 * 1024 * 1024
        ),
    )(index, lists, first, blocks)


def split(value):
    high = value.astype(jnp.bfloat16)
    rest = value - high.astype(jnp.float32)
    middle = rest.astype(jnp.bfloat16)
    return high, middle, (rest - middle.astype(jnp.float32)).astype(jnp.bfloat16)


def finish_kernel(gram_ref, rhs_ref, nat_ref, sol_ref, res_ref):
    size = S * NRHS
    gram = gram_ref[...]
    paired = gram[NRHS:] + gram[:size]
    lane = lax.broadcasted_iota(jnp.int32, (size, 128), 1)
    row = lax.broadcasted_iota(jnp.int32, (size, 128), 0)
    work = jnp.where(
        lane < size, paired + pltpu.roll(paired, 128 - NRHS, 1), pltpu.roll(paired, size, 1)
    )
    for k in range(size):
        line = work[k:k + 1]
        factor = jnp.where(row[:, :1] == k, 0.0, work[:, k:k + 1] * (1.0 / line[:, k:k + 1]))
        work = work - factor * line
    diagonal = jnp.sum(jnp.where(lane == row, work, 0.0), axis=1, keepdims=True)
    coef = pltpu.roll(work / diagonal, size, 1)
    coef = jnp.where(lane < NRHS, coef, 0.0)
    for step in (NRHS, 2 * NRHS, 4 * NRHS):
        coef = coef + pltpu.roll(coef, step, 1)
    zero = jnp.zeros((NRHS, 128), jnp.float32)
    parts = [coef[j * NRHS:(j + 1) * NRHS] for j in range(S)]
    for_sol = parts + [zero]
    for_res = [parts[0]] + [parts[j] + parts[j - 1] for j in range(1, S)] + [parts[S - 1]]
    group = lax.broadcasted_iota(jnp.int32, (128, 256), 0) // NRHS
    place = (lax.broadcasted_iota(jnp.int32, (128, 256), 1) % 128) // NRHS
    table = []
    for j in range(S + 1):
        both = jnp.concatenate([for_sol[j], for_res[j]], axis=1)
        table.append(jnp.where(group == place, jnp.concatenate([both] * 8, axis=0), 0.0))
    tables = split(jnp.concatenate(table, axis=0))
    for u in range(BS * NRHS // 128):
        lanes = slice(u * 128, (u + 1) * 128)
        first = rhs_ref[:, lanes]
        lhs = jnp.concatenate([first] + [nat_ref[j, :, lanes] for j in range(S)], axis=1)
        out = sum(jnp.dot(lhs, part, preferred_element_type=jnp.float32) for part in reversed(tables))
        sol_ref[:, lanes] = out[:, :128]
        res_ref[:, lanes] = first.astype(jnp.float32) - out[:, 128:]


def finish(gram, rhs, nat):
    shape = jax.ShapeDtypeStruct(rhs.shape, jnp.float32)
    return pl.pallas_call(
        finish_kernel,
        out_shape=(shape, shape),
        in_specs=[pl.BlockSpec(memory_space=pltpu.VMEM)] * 3,
        out_specs=[pl.BlockSpec(memory_space=pltpu.VMEM)] * 2,
        compiler_params=pltpu.CompilerParams(vmem_limit_bytes=24 * 1024 * 1024),
    )(gram, rhs, nat)


def on_device(rhs, blocks, columns, ghost_lists):
    n_space, n_sub = lax.axis_size("space"), lax.axis_size("sub")
    rows = rhs.shape[0]
    ghost = ghost_lists.shape[1] // 2
    q = lax.axis_index("sub")
    lists = ghost_lists[0]
    every = lax.all_gather(lists, "sub", axis=0)
    columns = columns.T
    near = columns[1:3]
    peer, row = near // rows, near % rows
    owner = jnp.arange(n_sub, dtype=jnp.int32)
    match = (peer[..., None, None] == owner[:, None]) & (row[..., None, None] == every[:, :ghost])
    place = jnp.sum(jnp.where(match, jnp.arange(ghost, dtype=jnp.int32), 0), axis=(2, 3))
    slot = (q - peer - 1) % n_sub
    near = jnp.where(peer == q, row, rows + slot * ghost + place)
    far = columns[3:] - n_sub * rows + rows + n_sub * ghost
    local = jnp.arange(rows, dtype=jnp.int32)[None]
    index = jnp.concatenate([local, near, far], axis=0)
    first = rhs.reshape(rows, BS, NRHS).transpose(0, 2, 1)
    first = jnp.concatenate([first, first], axis=2)
    gram, nat = powers(n_space, n_sub, index, lists, first, blocks.transpose(1, 0, 2))
    return finish(gram, rhs, nat)


def solution(mesh):
    in_specs = (
        P(("space", "sub"), None),
        P(("space", "sub"), None, None),
        P(("space", "sub"), None),
        P(("space", "sub"), None),
    )
    out_specs = (P(("space", "sub"), None), P(("space", "sub"), None))
    return jax.shard_map(
        on_device, mesh=mesh, in_specs=in_specs, out_specs=out_specs, check_vma=False
    )
```

```python
import functools

import jax
import jax.numpy as jnp
from jax import lax
from jax.experimental import pallas as pl
from jax.experimental.pallas import tpu as pltpu
from jax.sharding import PartitionSpec as P

BS = 64
NRHS = 16
NNZ = 7
S = 4
MESH = pl.DeviceIdType.MESH
NT = (((1,), (1,)), ((), ()))
CHUNKS = 4
BATCH = 32
PACK = 16


def log2(n):
    return n.bit_length() - 1


def powers_kernel(
    n_space, n_sub, rows, ghost,
    index_ref, list_ref, first_ref, blocks_ref,
    gram_ref, nat_ref,
    basis, lined, tall, perm, raw, mats, turn, ext, fresh, up, down, near, low, high, gsend, grecv,
    load_sem, send_sem, recv_sem, gsend_sem, grecv_sem,
):
    p = lax.axis_index("space")
    q = lax.axis_index("sub")
    half = ghost // 2
    pairs = rows // 2
    rounds_space = log2(n_space)
    has_low = p > 0
    flat = BS * NRHS
    has_high = p < n_space - 1

    per = rows // CHUNKS
    loads = [
        pltpu.make_async_copy(
            blocks_ref.at[:, pl.ds(n * per, per)], raw.at[:, pl.ds(n * per, per)], load_sem.at[n]
        )
        for n in range(CHUNKS)
    ]
    for load in loads:
        load.start()

    def flip(index, step):
        return index + step * (1 - 2 * ((index // step) % 2))

    barrier = pltpu.get_barrier_semaphore()
    for d in range(1, n_sub):
        pl.semaphore_signal(barrier, inc=1, device_id=(p, (q + d) % n_sub), device_id_type=MESH)
    for r in range(1, rounds_space):
        pl.semaphore_signal(barrier, inc=1, device_id=(flip(p, 1 << r), q), device_id_type=MESH)

    @pl.when(has_low)
    def _():
        pl.semaphore_signal(barrier, inc=1, device_id=(p - 1, q), device_id_type=MESH)

    @pl.when(has_high)
    def _():
        pl.semaphore_signal(barrier, inc=1, device_id=(p + 1, q), device_id_type=MESH)

    left16 = lax.broadcasted_iota(jnp.int32, (NRHS, 128), 1) < BS
    left32 = lax.broadcasted_iota(jnp.int32, (32, 128), 1) < BS
    src = lax.broadcasted_iota(jnp.int32, (128, 256), 0)
    dst = lax.broadcasted_iota(jnp.int32, (128, 256), 1)
    src_c = 2 * (src % 32) + (src // 32) % 2
    order = jnp.where((src // BS == dst // 128) & (src_c == dst % BS), 1.0, 0.0).astype(jnp.bfloat16)
    double = jnp.where((src // BS == dst // 128) & (src % BS == dst % BS), 1.0, 0.0).astype(jnp.bfloat16)

    def own_start(m, carry):
        even, odd = first_ref[2 * m], first_ref[2 * m + 1]
        ext[2 * m] = even
        ext[2 * m + 1] = odd
        basis[0, m] = jnp.where(left16, even, odd)
        return carry

    lax.fori_loop(0, pairs, own_start, 0)

    def zero(m, carry):
        ext[rows + n_sub * ghost + m] = jnp.zeros((NRHS, 128), jnp.bfloat16)
        return carry

    lax.fori_loop(0, 2 * ghost, zero, 0)

    def copies(j):
        near_copies = [
            pltpu.make_async_remote_copy(
                src_ref=up.at[j], dst_ref=near.at[j, d - 1],
                send_sem=send_sem.at[j, d - 1], recv_sem=recv_sem.at[j, d - 1],
                device_id=(p, (q + d) % n_sub), device_id_type=MESH,
            )
            for d in range(1, n_sub)
        ]
        up_copy = pltpu.make_async_remote_copy(
            src_ref=up.at[j], dst_ref=low.at[j],
            send_sem=send_sem.at[j, n_sub - 1], recv_sem=recv_sem.at[j, n_sub - 1],
            device_id=((p + 1) % n_space, q), device_id_type=MESH,
        )
        down_copy = pltpu.make_async_remote_copy(
            src_ref=down.at[j], dst_ref=high.at[j],
            send_sem=send_sem.at[j, n_sub], recv_sem=recv_sem.at[j, n_sub],
            device_id=((p + n_space - 1) % n_space, q), device_id_type=MESH,
        )
        return near_copies, up_copy, down_copy

    def send(j):
        near_copies, up_copy, down_copy = copies(j)

        def pack(target, start):
            def body(m, carry):
                taken = [
                    jnp.where(
                        left16,
                        ext[list_ref[start + 2 * (PACK * m + u)]],
                        ext[list_ref[start + 2 * (PACK * m + u) + 1]],
                    )
                    for u in range(PACK)
                ]
                for u in range(PACK):
                    target[j, PACK * m + u] = taken[u]
                return carry

            lax.fori_loop(0, half // PACK, body, 0)

        pack(up, 0)
        if j == 0:
            greeted = (n_sub - 1) + (rounds_space - 1)
            pl.semaphore_wait(barrier, greeted + jnp.where(has_low, 1, 0) + jnp.where(has_high, 1, 0))
        pl.when(has_high)(up_copy.start)
        for copy in near_copies:
            copy.start()
        pack(down, ghost)
        pl.when(has_low)(down_copy.start)

    def spread(buffer, lead, base):
        part = buffer[lead].reshape(half * NRHS, 128)
        wide = jnp.dot(part, double, preferred_element_type=jnp.float32).astype(jnp.bfloat16)
        for h in range(half):
            ext[base + 2 * h] = wide[h * NRHS:(h + 1) * NRHS, :128]
            ext[base + 2 * h + 1] = wide[h * NRHS:(h + 1) * NRHS, 128:]

    def receive(j):
        near_copies, up_copy, down_copy = copies(j)
        for d, copy in enumerate(near_copies):
            copy.wait_recv()
            spread(near, (j, d), rows + d * ghost)

        @pl.when(has_low)
        def _():
            up_copy.wait_recv()
            spread(low, (j,), rows + n_sub * ghost)

        @pl.when(has_high)
        def _():
            down_copy.wait_recv()
            spread(high, (j,), rows + n_sub * ghost + ghost)

    def sent(j):
        near_copies, up_copy, down_copy = copies(j)
        for copy in near_copies:
            copy.wait_send()
        pl.when(has_high)(up_copy.wait_send)
        pl.when(has_low)(down_copy.wait_send)

    def relay(g, carry):
        base = pl.multiple_of(g * 16, 16)
        for m in range(4):
            members = [b for b in (2 * m, 2 * m + 1) if b < NNZ]
            for b in members:
                for t in range(32):
                    turn[b % 2, t * 16:(t + 1) * 16, :] = raw[
                        b, pl.ds(base, 16), t * 128:(t + 1) * 128
                    ].astype(jnp.float32)
            for u in range(16):
                planes = [turn[b % 2, pl.ds(u, 32, stride=16), :] for b in members]
                swapped = [pltpu.roll(plane, BS, 1) for plane in planes]
                if len(members) < 2:
                    planes.append(jnp.zeros((32, 128), jnp.float32))
                    swapped.append(planes[1])
                lanes = slice(m * 128, (m + 1) * 128)
                mats[base + u, 0:32, lanes] = jnp.where(left32, planes[0], swapped[1]).astype(jnp.bfloat16)
                mats[base + u, 32:64, lanes] = jnp.where(left32, swapped[0], planes[1]).astype(jnp.bfloat16)
        return carry

    def picks(at, count):
        lines = []
        for u in range(count):
            tiles = [ext[index_ref[b, at + u]] for b in range(NNZ)]
            lines.append(jnp.concatenate(
                [jnp.where(left16, tiles[2 * m], tiles[2 * m + 1]) for m in range(3)] + [tiles[6]], axis=1
            ))
        return jnp.concatenate(lines, axis=0)

    def product(j):
        def body(g, carry):
            start = BATCH * g
            lhs = [picks(start + 4 * n, 4) for n in range(BATCH // 4)]
            picked = []
            for n in range(BATCH // 4):
                block = mats[pl.ds(start + 4 * n, 4)].reshape(4 * BS, 512)
                full = lax.dot_general(lhs[n], block, NT, preferred_element_type=jnp.float32)
                for h in range(2):
                    picked.append(jnp.where(
                        left16,
                        full[2 * h * NRHS:(2 * h + 1) * NRHS, h * 128:(h + 1) * 128],
                        full[(2 * h + 1) * NRHS:(2 * h + 2) * NRHS, h * 128:(h + 1) * 128],
                    ).astype(jnp.bfloat16))
            wide = jnp.dot(
                jnp.concatenate(picked, axis=0), order, preferred_element_type=jnp.float32
            ).astype(jnp.bfloat16)
            for h in range(BATCH // 2):
                even = wide[h * NRHS:(h + 1) * NRHS, :128]
                odd = wide[h * NRHS:(h + 1) * NRHS, 128:]
                fresh[start + 2 * h] = even
                fresh[start + 2 * h + 1] = odd
                basis[j + 1, BATCH // 2 * g + h] = jnp.where(left16, even, odd)
            return carry

        lax.fori_loop(0, rows // BATCH, body, 0)

        if j < S - 1:
            ext[pl.ds(0, rows)] = fresh[...]

    def natural(j):
        def line(m, carry):
            base = pl.multiple_of(m * 32, 32)
            tall[...] = fresh[pl.ds(base, 32)].reshape(32 * NRHS, 128).astype(jnp.float32)
            planes = [tall[pl.ds(k, 32, stride=NRHS), :] for k in range(NRHS)]
            for k in range(NRHS // 2):
                lined[pl.ds(base, 32), k * 128:(k + 1) * 128] = jnp.where(
                    left32, planes[2 * k], planes[2 * k + 1]
                ).astype(jnp.bfloat16)
            return carry

        lax.fori_loop(0, rows // 32, line, 0)
        for n in range(flat // 256):
            lanes = slice(n * 256, (n + 1) * 256)
            nat_ref[j, :, lanes] = jnp.dot(
                lined[...], perm[:, lanes], preferred_element_type=jnp.float32
            ).astype(jnp.bfloat16)

    def permutation(k, carry):
        at = lax.broadcasted_iota(jnp.int32, (BS, flat), 1)
        c = lax.broadcasted_iota(jnp.int32, (BS, flat), 0)
        perm[pl.ds(pl.multiple_of(k * BS, BS), BS), :] = jnp.where(
            at == c * NRHS + k, 1.0, 0.0
        ).astype(jnp.bfloat16)
        return carry

    for j in range(S):
        send(j)
        if j == 1:
            lax.fori_loop(0, NRHS, permutation, 0)
        if j >= 1:
            natural(j - 1)
        if j == 0:
            for n in range(CHUNKS):
                loads[n].wait()
                lax.fori_loop(n * per // 16, (n + 1) * per // 16, relay, 0)
        receive(j)
        product(j)
        sent(j)

    width = (S + 1) * NRHS

    def gram_step(m, total):
        tile = jnp.concatenate(
            [basis[:, 8 * m + h].reshape(width, 128) for h in range(8)], axis=1
        )
        return total + lax.dot_general(tile, tile, NT, preferred_element_type=jnp.float32)

    total = lax.fori_loop(0, pairs // 8, gram_step, jnp.zeros((width, width), jnp.float32), unroll=2)
    gsend[...] = jnp.zeros_like(gsend)
    gsend[0, :, :width] = total
    peers = [
        pltpu.make_async_remote_copy(
            src_ref=gsend.at[0], dst_ref=grecv.at[d - 1],
            send_sem=gsend_sem.at[d - 1], recv_sem=grecv_sem.at[d - 1],
            device_id=(p, (q + d) % n_sub), device_id_type=MESH,
        )
        for d in range(1, n_sub)
    ]
    for copy in peers:
        copy.start()
    natural(S - 1)
    value = gsend[0]
    for d, copy in enumerate(peers):
        copy.wait()
        value = value + grecv[d]
    for r in range(rounds_space):
        at = n_sub - 1 + r
        gsend[r + 1] = value
        copy = pltpu.make_async_remote_copy(
            src_ref=gsend.at[r + 1], dst_ref=grecv.at[at],
            send_sem=gsend_sem.at[at], recv_sem=grecv_sem.at[at],
            device_id=(flip(p, 1 << r), q), device_id_type=MESH,
        )
        copy.start()
        copy.wait()
        value = value + grecv[at]
    gram_ref[...] = value


def powers(n_space, n_sub, index, lists, first, blocks):
    rows = blocks.shape[1]
    ghost = lists.shape[0] // 2
    half = ghost // 2
    width = (S + 1) * NRHS
    rounds = n_sub - 1 + log2(n_space)
    bf, f32 = jnp.bfloat16, jnp.float32
    return pl.pallas_call(
        functools.partial(powers_kernel, n_space, n_sub, rows, ghost),
        out_shape=(
            jax.ShapeDtypeStruct((width, 128), f32),
            jax.ShapeDtypeStruct((S, rows, BS * NRHS), bf),
        ),
        in_specs=[
            pl.BlockSpec(memory_space=pltpu.SMEM),
            pl.BlockSpec(memory_space=pltpu.SMEM),
            pl.BlockSpec(memory_space=pltpu.VMEM),
            pl.BlockSpec(memory_space=pl.ANY),
        ],
        out_specs=[pl.BlockSpec(memory_space=pltpu.VMEM)] * 2,
        scratch_shapes=[
            pltpu.VMEM((S + 1, rows // 2, NRHS, 128), bf),
            pltpu.VMEM((rows, BS * NRHS), bf),
            pltpu.VMEM((32 * NRHS, 128), f32),
            pltpu.VMEM((BS * NRHS, BS * NRHS), bf),
            pltpu.VMEM((NNZ, rows, BS * BS), bf),
            pltpu.VMEM((rows, BS, 512), bf),
            pltpu.VMEM((2, 512, 128), f32),
            pltpu.VMEM((rows + n_sub * ghost + 2 * ghost, NRHS, 128), bf),
            pltpu.VMEM((rows, NRHS, 128), bf),
            pltpu.VMEM((S, half, NRHS, 128), bf),
            pltpu.VMEM((S, half, NRHS, 128), bf),
            pltpu.VMEM((S, n_sub - 1, half, NRHS, 128), bf),
            pltpu.VMEM((S, half, NRHS, 128), bf),
            pltpu.VMEM((S, half, NRHS, 128), bf),
            pltpu.VMEM((rounds, width, 128), f32),
            pltpu.VMEM((rounds, width, 128), f32),
            pltpu.SemaphoreType.DMA((CHUNKS,)),
            pltpu.SemaphoreType.DMA((S, n_sub + 1)),
            pltpu.SemaphoreType.DMA((S, n_sub + 1)),
            pltpu.SemaphoreType.DMA((rounds,)),
            pltpu.SemaphoreType.DMA((rounds,)),
        ],
        compiler_params=pltpu.CompilerParams(
            collective_id=0, has_side_effects=True, vmem_limit_bytes=56 * 1024 * 1024
        ),
    )(index, lists, first, blocks)


def split(value):
    high = value.astype(jnp.bfloat16)
    rest = value - high.astype(jnp.float32)
    middle = rest.astype(jnp.bfloat16)
    return high, middle, (rest - middle.astype(jnp.float32)).astype(jnp.bfloat16)


def finish_kernel(gram_ref, rhs_ref, nat_ref, sol_ref, res_ref):
    size = S * NRHS
    gram = gram_ref[...]
    paired = gram[NRHS:] + gram[:size]
    lane = lax.broadcasted_iota(jnp.int32, (size, 128), 1)
    row = lax.broadcasted_iota(jnp.int32, (size, 128), 0)
    work = jnp.where(
        lane < size, paired + pltpu.roll(paired, 128 - NRHS, 1), pltpu.roll(paired, size, 1)
    )
    for k in range(size):
        line = work[k:k + 1]
        factor = jnp.where(row[:, :1] == k, 0.0, work[:, k:k + 1] * (1.0 / line[:, k:k + 1]))
        work = work - factor * line
    diagonal = jnp.sum(jnp.where(lane == row, work, 0.0), axis=1, keepdims=True)
    coef = pltpu.roll(work / diagonal, size, 1)
    coef = jnp.where(lane < NRHS, coef, 0.0)
    for step in (NRHS, 2 * NRHS, 4 * NRHS):
        coef = coef + pltpu.roll(coef, step, 1)
    zero = jnp.zeros((NRHS, 128), jnp.float32)
    parts = [coef[j * NRHS:(j + 1) * NRHS] for j in range(S)]
    for_sol = parts + [zero]
    for_res = [parts[0]] + [parts[j] + parts[j - 1] for j in range(1, S)] + [parts[S - 1]]
    group = lax.broadcasted_iota(jnp.int32, (128, 256), 0) // NRHS
    place = (lax.broadcasted_iota(jnp.int32, (128, 256), 1) % 128) // NRHS
    table = []
    for j in range(S + 1):
        both = jnp.concatenate([for_sol[j], for_res[j]], axis=1)
        table.append(jnp.where(group == place, jnp.concatenate([both] * 8, axis=0), 0.0))
    tables = split(jnp.concatenate(table, axis=0))
    for u in range(BS * NRHS // 128):
        lanes = slice(u * 128, (u + 1) * 128)
        first = rhs_ref[:, lanes]
        lhs = jnp.concatenate([first] + [nat_ref[j, :, lanes] for j in range(S)], axis=1)
        out = sum(jnp.dot(lhs, part, preferred_element_type=jnp.float32) for part in reversed(tables))
        sol_ref[:, lanes] = out[:, :128]
        res_ref[:, lanes] = first.astype(jnp.float32) - out[:, 128:]


def finish(gram, rhs, nat):
    shape = jax.ShapeDtypeStruct(rhs.shape, jnp.float32)
    return pl.pallas_call(
        finish_kernel,
        out_shape=(shape, shape),
        in_specs=[pl.BlockSpec(memory_space=pltpu.VMEM)] * 3,
        out_specs=[pl.BlockSpec(memory_space=pltpu.VMEM)] * 2,
        compiler_params=pltpu.CompilerParams(vmem_limit_bytes=24 * 1024 * 1024),
    )(gram, rhs, nat)


def on_device(rhs, blocks, columns, ghost_lists):
    n_space, n_sub = lax.axis_size("space"), lax.axis_size("sub")
    rows = rhs.shape[0]
    ghost = ghost_lists.shape[1] // 2
    q = lax.axis_index("sub")
    lists = ghost_lists[0]
    every = lax.all_gather(lists, "sub", axis=0)
    columns = columns.T
    near = columns[1:3]
    peer, row = near // rows, near % rows
    owner = jnp.arange(n_sub, dtype=jnp.int32)
    match = (peer[..., None, None] == owner[:, None]) & (row[..., None, None] == every[:, :ghost])
    place = jnp.sum(jnp.where(match, jnp.arange(ghost, dtype=jnp.int32), 0), axis=(2, 3))
    slot = (q - peer - 1) % n_sub
    near = jnp.where(peer == q, row, rows + slot * ghost + place)
    far = columns[3:] - n_sub * rows + rows + n_sub * ghost
    local = jnp.arange(rows, dtype=jnp.int32)[None]
    index = jnp.concatenate([local, near, far], axis=0)
    first = rhs.reshape(rows, BS, NRHS).transpose(0, 2, 1)
    first = jnp.concatenate([first, first], axis=2)
    gram, nat = powers(n_space, n_sub, index, lists, first, blocks.transpose(1, 0, 2))
    return finish(gram, rhs, nat)


def solution(mesh):
    in_specs = (
        P(("space", "sub"), None),
        P(("space", "sub"), None, None),
        P(("space", "sub"), None),
        P(("space", "sub"), None),
    )
    out_specs = (P(("space", "sub"), None), P(("space", "sub"), None))
    return jax.shard_map(
        on_device, mesh=mesh, in_specs=in_specs, out_specs=out_specs, check_vma=False
    )
```
